256 devices in a mesh: depth: 8 (over z_hi, core), tile: 32 (over y, x, z_lo).
Axes of the slice: x: 4, y: 4, z: 8 (z_hi: 4, z_lo: 2; z = z_hi * 2 + z_lo), core: 2. Of those that a mesh axis runs over, the one named last changes fastest.
Arguments:
- surface: float32 [4, 2, 2, 4, 1024, 128], P(None, None, None, None, 'tile'), may hold values from -5 to 5
- speeds: int32 [16, 1024, 128], P('depth', 'tile'), may hold values from 0 to 127
- table: float32 [16, 2, 8, 128], replicated, may hold values from -1 to 1
Outputs:
- image: float32 [16, 1024, 128], P('depth', 'tile')
The draws below stay inside these ranges and needn't reach their ends.
All inputs are finite; a program needn't handle non-finite values.
Results may differ from the reference program's by a relative error of at most 0.0003.
Values sent between devices are 32-bit elements; how exact they have to be, the bound alone decides.
A program may use at most 64 MiB of HBM per device.

```python
import math
import jax
import jax.numpy as jnp
from jax import lax

NY = 128
F = 4
MB = 4
TERMS = 8
NV = 128
NX = 1024
LEVELS = 16
FREQS = 16


def draw_surface(key, part):
    key = jax.random.fold_in(key, 7)
    shape = (MB, 2, 2, F, NX, NY)
    return jax.random.truncated_normal(key, -5.0, 5.0, shape, jnp.float32)


def draw_table(key, part):
    key = jax.random.fold_in(key, 11)
    first, second = jax.random.split(key)
    shape = (FREQS, 1, TERMS, NV)
    leading = (lax.broadcasted_iota(jnp.int32, shape, 2) == 0).astype(jnp.float32)
    spread = jax.random.uniform(first, shape, jnp.float32, 0.0, 1.0)
    modulus = leading * (0.7 + 0.25 * spread) + (1.0 - leading) * (0.1 + 0.25 * spread)
    phase = jax.random.uniform(second, shape, jnp.float32, -math.pi, math.pi)
    return jnp.concatenate([modulus * jnp.cos(phase), modulus * jnp.sin(phase)], axis=1)


def plant(drawn, own_key, least, high):
    index_at = [jax.random.randint(jax.random.fold_in(own_key, axis), (), 0, length) for axis, length in enumerate(drawn.shape)]
    main_axis = drawn.shape.index(max(drawn.shape))
    neighbour = index_at[:main_axis] + [(index_at[main_axis] + 1) % drawn.shape[main_axis]] + index_at[main_axis + 1:]
    return drawn.at[tuple(index_at)].set(least).at[tuple(neighbour)].set(high)


def setup_inputs(seed: int = 0) -> dict:
    key_of = jax.random.split(jax.random.key(seed), 4)
    surface = draw_surface(jax.random.fold_in(key_of[3], 71), 0)
    speeds = plant(jax.random.randint(key_of[1], (LEVELS, NX, NY), 0, NV), jax.random.fold_in(key_of[1], 1), 0, NV - 1).astype(jnp.int32)
    table = draw_table(jax.random.fold_in(key_of[3], 71), 0)
    return dict(surface=surface, speeds=speeds, table=table)


def mcclellan(field):
    lead = [(0, 0)] * (field.ndim - 2)
    padded = jnp.pad(field, lead + [(1, 1), (0, 0)])
    along_rows = field + 0.5 * (padded[..., 2:, :] + padded[..., :-2, :])
    padded = jnp.pad(along_rows, lead + [(0, 0), (1, 1)])
    along_columns = along_rows + 0.5 * (padded[..., :, 2:] + padded[..., :, :-2])
    return 0.5 * along_columns - field


def accumulate(totals, term, factors, index):
    cosine = factors[:, 0, index]
    sine = factors[:, 1, index]
    src_re = totals[0] + cosine * term[0, 0] - sine * term[0, 1]
    src_im = totals[1] + cosine * term[0, 1] + sine * term[0, 0]
    rec_re = totals[2] + cosine * term[1, 0] + sine * term[1, 1]
    rec_im = totals[3] + cosine * term[1, 1] - sine * term[1, 0]
    return (src_re, src_im, rec_re, rec_im)


def chebyshev_sum(fields, factors):
    terms = factors.shape[2]
    zero = jnp.zeros(factors[:, 0, 0].shape, jnp.float32)
    totals = accumulate((zero, zero, zero, zero), fields, factors, 0)
    older = fields
    newer = mcclellan(fields)
    totals = accumulate(totals, newer, factors, 1)
    for index in range(2, terms):
        older, newer = newer, 2.0 * mcclellan(newer) - older
        totals = accumulate(totals, newer, factors, index)
    return jnp.stack([jnp.stack([totals[0], totals[1]]), jnp.stack([totals[2], totals[3]])])


def correlate(fields):
    return jnp.sum(fields[0, 0] * fields[1, 0] + fields[0, 1] * fields[1, 1], axis=0)


def reference(surface, speeds, table):
    fields = [surface[batch] for batch in range(MB)]
    layers = []
    for level in range(LEVELS):
        total = jnp.zeros((NX, NY), jnp.float32)
        for batch in range(MB):
            block = table[batch * F:(batch + 1) * F]
            factors = block[:, :, :, speeds[level]]
            fields[batch] = chebyshev_sum(fields[batch], factors)
            total = total + correlate(fields[batch])
        layers.append(total)
    return jnp.stack(layers)
```

```python
import functools

import jax
import jax.numpy as jnp
from jax import lax
from jax.experimental import pallas as pl
from jax.experimental.pallas import tpu as pltpu
from jax.sharding import PartitionSpec as P

MESH = pl.DeviceIdType.MESH
TERMS = 8
BLOCK = 4
TILE = 32
HALO = 32
EXT = 128
PAD = 8
CHUNK = 32


def chebyshev_in_powers():
    rows = [[1], [0, 1]]
    for _ in range(2, TERMS):
        up = [0] + [2 * v for v in rows[-1]]
        old = rows[-2] + [0] * (len(up) - len(rows[-2]))
        rows.append([a - b for a, b in zip(up, old)])
    return rows


def pieces(low, high):
    cuts = {low, high}
    for edge in (24, 32, 96, 104):
        if low < edge < high:
            cuts.add(edge)
    marks = sorted(cuts)
    out = []
    for start, stop in zip(marks[:-1], marks[1:]):
        while start < stop:
            size = min(CHUNK, stop - start)
            out.append((start, size))
            start += size
    return out


def kernel(
    surface, speeds, table, out,
    planes, speed_all, tab, partial, landed, halo,
    local_sem, field_send, field_recv, edge_send, edge_recv,
    gather_send, gather_recv, relay_send, halo_send, halo_recv, image_send, image_recv,
):
    s = lax.axis_index("depth")
    t = lax.axis_index("tile")
    columns = lax.axis_size("tile") // 2
    col, zl = t // 2, t % 2
    zh, core = s // 2, s % 2
    z = zh * 2 + zl
    sibling = zh * 2 + (1 - core)
    outward = jnp.where(zl == 0, t - 1, t + 1)
    beyond = jnp.where(zl == 0, t - 2, t + 2)
    has_out = jnp.where(zl == 0, col > 0, col < columns - 1)
    has_left = col > 0
    has_right = col < columns - 1
    has_in = jnp.where(zl == 0, has_right, has_left)
    inward = jnp.where(zl == 0, t + 2, t - 2)

    def chip(step):
        other = (z + step) % 8
        return other // 2, other % 2

    @pl.when(jnp.logical_not(has_left))
    def _():
        planes[0, :, PAD : PAD + HALO, :] = jnp.zeros((4, HALO, 128), jnp.float32)
        speed_all[:, 0:HALO, :] = jnp.zeros((16, HALO, 128), jnp.int32)

    @pl.when(jnp.logical_not(has_right))
    def _():
        planes[0, :, PAD + EXT - HALO : PAD + EXT, :] = jnp.zeros((4, HALO, 128), jnp.float32)
        speed_all[:, EXT - HALO : EXT, :] = jnp.zeros((16, HALO, 128), jnp.int32)

    barrier = pltpu.get_barrier_semaphore()

    def greet(depth, tile):
        pl.semaphore_signal(barrier, inc=1, device_id=(depth, tile), device_id_type=MESH)

    greet(sibling, t)
    for step in range(1, 8):
        ozh, ozl = chip(step)
        greet(ozh * 2, 2 * col + ozl)
        greet(ozh * 2 + 1, 2 * col + ozl)

    @pl.when(has_out)
    def _():
        greet(s, outward)
        greet(s, beyond)

    @pl.when(has_in)
    def _():
        greet(s, inward)

    freq = s * 2 + zl
    coef = chebyshev_in_powers()
    for part in range(2):
        for power in range(TERMS):
            row = None
            for n in range(power, TERMS):
                c = coef[n][power]
                if c:
                    term = table[freq, part, n : n + 1, :] * (c / 8.0**power)
                    row = term if row is None else row + term
            tab[part * TERMS + power] = jnp.broadcast_to(row, (8, 128))

    pl.semaphore_wait(
        barrier, 15 + 2 * has_out.astype(jnp.int32) + has_in.astype(jnp.int32)
    )

    own_row = HALO + TILE * zl
    far_row = jnp.where(zl == 0, EXT - HALO, 0)

    def edge_copy():
        return pltpu.make_async_remote_copy(
            src_ref=speeds,
            dst_ref=speed_all.at[pl.ds(2 * s, 2), pl.ds(pl.multiple_of(far_row, 32), TILE), :],
            send_sem=edge_send,
            recv_sem=edge_recv,
            device_id=(s, outward),
            device_id_type=MESH,
        )

    @pl.when(has_out)
    def _():
        edge_copy().start()

    own_speed = pltpu.make_async_copy(
        speeds,
        speed_all.at[pl.ds(2 * s, 2), pl.ds(pl.multiple_of(own_row, 32), TILE), :],
        local_sem.at[0],
    )
    own_speed.start()

    def field_copy(target, target_zl, slot, sem):
        wanted = s * 2 + target_zl
        return pltpu.make_async_remote_copy(
            src_ref=surface.at[wanted // 4, :, wanted % 4],
            dst_ref=planes.at[0].at[:, pl.ds(pl.multiple_of(PAD + TILE * slot, 8), TILE), :],
            send_sem=field_send.at[sem],
            recv_sem=field_recv.at[slot],
            device_id=(s, target),
            device_id_type=MESH,
        )

    field_copy(2 * col + 1 - zl, 1 - zl, 1 + zl, 0).start()

    @pl.when(has_out)
    def _():
        slot = jnp.where(zl == 0, 3, 0)
        field_copy(outward, 1 - zl, slot, 1).start()
        field_copy(beyond, zl, slot, 2).start()

    own_field = pltpu.make_async_copy(
        surface.at[freq // 4, :, freq % 4],
        planes.at[0].at[:, pl.ds(pl.multiple_of(PAD + own_row, 8), TILE), :],
        local_sem.at[1],
    )
    own_field.start()

    own_speed.wait()

    @pl.when(has_out)
    def _():
        edge_copy().wait()

    def span(lev, who):
        rows = TILE + 24 - 8 * lev
        return jnp.where(who == 0, HALO + TILE - rows, HALO + TILE), rows

    def level_copy(level, lev, who, target, send):
        first, rows = span(lev, who)
        part = speed_all.at[level, pl.ds(pl.multiple_of(first, 8), rows), :]
        return pltpu.make_async_remote_copy(
            src_ref=part,
            dst_ref=part,
            send_sem=send,
            recv_sem=gather_recv.at[level, who],
            device_id=target,
            device_id_type=MESH,
        )

    for lev in range(2):
        for step in range(1, 8):
            ozh, ozl = chip(step)
            level_copy(
                2 * s + lev, lev, zl, (ozh * 2 + core, 2 * col + ozl), gather_send.at[lev, step]
            ).start()
        level_copy(2 * s + lev, lev, zl, (sibling, t), relay_send.at[lev, 0]).start()
    for step in range(7, 0, -1):
        ozh, ozl = chip(step)
        for lev in range(2):
            level = 2 * (ozh * 2 + core) + lev
            level_copy(level, lev, ozl, (sibling, t), gather_send.at[lev, step]).wait_recv()
            level_copy(level, lev, ozl, (sibling, t), relay_send.at[lev, step]).start()
    for step in range(8):
        ozh, ozl = chip(step)
        for lev in range(2):
            level = 2 * (ozh * 2 + 1 - core) + lev
            level_copy(level, lev, ozl, (sibling, t), relay_send.at[lev, step]).wait_recv()

    own_field.wait()
    field_copy(2 * col + 1 - zl, 1 - zl, 1 + zl, 0).wait_send()
    field_copy(2 * col + 1 - zl, 1 - zl, 2 - zl, 0).wait_recv()

    @pl.when(has_out)
    def _():
        slot = jnp.where(zl == 0, 3, 0)
        field_copy(outward, 1 - zl, slot, 1).wait_send()
        field_copy(beyond, zl, slot, 2).wait_send()

    @pl.when(has_left)
    def _():
        field_copy(t, 1 - zl, 0, 1).wait_recv()

    @pl.when(has_right)
    def _():
        field_copy(t, 1 - zl, 3, 1).wait_recv()

    for lev in range(2):
        for step in range(1, 8):
            level_copy(2 * s + lev, lev, zl, (sibling, t), gather_send.at[lev, step]).wait_send()
        for step in range(8):
            level_copy(2 * s + lev, lev, zl, (sibling, t), relay_send.at[lev, step]).wait_send()

    lane = lax.broadcasted_iota(jnp.int32, (CHUNK, 128), 1)
    first_lane, last_lane = lane == 0, lane == 127
    sub = lax.broadcasted_iota(jnp.int32, (8, 128), 0)
    top_wall = (sub == 7) & jnp.logical_not(has_left)
    low_wall = (sub == 0) & jnp.logical_not(has_right)

    def image_copy(level, half):
        return pltpu.make_async_remote_copy(
            src_ref=partial.at[level, pl.ds(pl.multiple_of(TILE * half, 32), TILE), :],
            dst_ref=landed.at[level % 2, freq],
            send_sem=image_send.at[level, half],
            recv_sem=image_recv.at[level % 2, freq],
            device_id=(level // 2, 2 * col + half),
            device_id_type=MESH,
        )

    def mine(level, half):
        return (level // 2 == s) & (half == zl)

    def halo_copy(block, side):
        return pltpu.make_async_remote_copy(
            src_ref=planes.at[0].at[:, pl.ds(PAD + HALO + TILE * side, TILE), :],
            dst_ref=halo.at[block, 1 - side],
            send_sem=halo_send.at[block, side],
            recv_sem=halo_recv.at[block, 1 - side],
            device_id=(s, t - 2 + 4 * side),
            device_id_type=MESH,
        )

    def run_block(block, carry):
        for lev in range(BLOCK):
            low = 8 * (lev + 1)
            high = EXT - low
            level = block * BLOCK + lev

            def stencil(n, c):
                for p in range(4):
                    for r, size in pieces(low - 8, high + 8):
                        w = planes[n, p, PAD + r : PAD + r + size, :]
                        u = planes[n, p, PAD + r - 1 : PAD + r + size - 1, :]
                        d = planes[n, p, PAD + r + 1 : PAD + r + size + 1, :]
                        x = (u + d) + (w + w)
                        left = jnp.where(first_lane[:size], 0.0, pltpu.roll(x, 1, 1))
                        right = jnp.where(last_lane[:size], 0.0, pltpu.roll(x, 127, 1))
                        g = ((x + x) - 8.0 * w) + (left + right)
                        if r == 24:
                            g = jnp.where(top_wall, 0.0, g)
                        if r == 96:
                            g = jnp.where(low_wall, 0.0, g)
                        planes[n + 1, p, PAD + r : PAD + r + size, :] = g
                return c

            lax.fori_loop(0, TERMS - 1, stencil, 0)
            for r in range(low, high, 8):
                index = speed_all[level, r : r + 8, :]
                total = None
                for n in range(TERMS):
                    cos = jnp.take_along_axis(tab[n], index, axis=1, mode="promise_in_bounds")
                    sin = jnp.take_along_axis(
                        tab[TERMS + n], index, axis=1, mode="promise_in_bounds"
                    )
                    a, b, c, d = (planes[n, p, PAD + r : PAD + r + 8, :] for p in range(4))
                    new = (
                        cos * a - sin * b,
                        cos * b + sin * a,
                        cos * c + sin * d,
                        cos * d - sin * c,
                    )
                    total = new if n == 0 else tuple(o + v for o, v in zip(total, new))
                for p in range(4):
                    planes[0, p, PAD + r : PAD + r + 8, :] = total[p]
                if HALO <= r < EXT - HALO:
                    partial[level, r - HALO : r - HALO + 8, :] = (
                        total[0] * total[2] + total[1] * total[3]
                    )
            for half in range(2):

                @pl.when(jnp.logical_not(mine(level, half)))
                def _():
                    image_copy(level, half).start()

        @pl.when(block < 3)
        def _():
            for side, there in ((0, has_left), (1, has_right)):

                @pl.when(there)
                def _():
                    halo_copy(block, side).start()

            for side, there in ((0, has_left), (1, has_right)):

                @pl.when(there)
                def _():
                    halo_copy(block, side).wait_send()
                    halo_copy(block, 1 - side).wait_recv()
                    base = PAD + (EXT - HALO) * side
                    planes[0, :, base : base + HALO, :] = halo[block, side]

        return carry

    lax.fori_loop(0, 16 // BLOCK, run_block, 0)

    for lev in range(2):
        total = partial[2 * s + lev, pl.ds(pl.multiple_of(TILE * zl, 32), TILE), :]
        for step in range(8):
            ozh, ozl = chip(step)
            for c in range(2):
                if step == 0 and c == 1:
                    continue
                src = (ozh * 2 + (core if c == 0 else 1 - core)) * 2 + ozl
                if step == 0:
                    src = sibling * 2 + zl
                pltpu.make_async_remote_copy(
                    src_ref=partial.at[0, pl.ds(0, TILE), :],
                    dst_ref=landed.at[lev, src],
                    send_sem=image_send.at[0, 0],
                    recv_sem=image_recv.at[lev, src],
                    device_id=(s, t),
                    device_id_type=MESH,
                ).wait_recv()
                total = total + landed[lev, src]
        out[lev] = total

    def drain(level, carry):
        for half in range(2):

            @pl.when(jnp.logical_not(mine(level, half)))
            def _():
                image_copy(level, half).wait_send()

        return carry

    lax.fori_loop(0, 16, drain, 0)


def body(surface, speeds, table):
    vmem = pl.BlockSpec(memory_space=pltpu.VMEM)
    dma = pltpu.SemaphoreType.DMA
    return pl.pallas_call(
        kernel,
        out_shape=jax.ShapeDtypeStruct((2, TILE, 128), jnp.float32),
        in_specs=[pl.BlockSpec(memory_space=pl.ANY), vmem, vmem],
        out_specs=vmem,
        scratch_shapes=[
            pltpu.VMEM((TERMS, 4, EXT + 2 * PAD, 128), jnp.float32),
            pltpu.VMEM((16, EXT, 128), jnp.int32),
            pltpu.VMEM((2 * TERMS, 8, 128), jnp.float32),
            pltpu.VMEM((16, 2 * TILE, 128), jnp.float32),
            pltpu.VMEM((2, 16, TILE, 128), jnp.float32),
            pltpu.VMEM((3, 2, 4, HALO, 128), jnp.float32),
            dma((2,)),
            dma((3,)),
            dma((4,)),
            dma,
            dma,
            dma((2, 8)),
            dma((16, 2)),
            dma((2, 8)),
            dma((3, 2)),
            dma((3, 2)),
            dma((16, 2)),
            dma((2, 16)),
        ],
        compiler_params=pltpu.CompilerParams(
            collective_id=0, has_side_effects=True, vmem_limit_bytes=32 << 20
        ),
    )(surface, speeds, table)


def solution(mesh):
    def flat(surface, speeds, table):
        return body(surface.reshape(4, 4, 4, TILE, 128), speeds, table)

    return jax.shard_map(
        flat,
        mesh=mesh,
        in_specs=(P(None, None, None, None, "tile", None), P("depth", "tile", None), P()),
        out_specs=P("depth", "tile", None),
        check_vma=False,
    )
```

```python
import jax
import jax.numpy as jnp
from jax import lax
from jax.experimental import pallas as pl
from jax.experimental.pallas import tpu as pltpu
from jax.sharding import PartitionSpec as P

MESH = pl.DeviceIdType.MESH
TERMS = 8
LEVELS = 16
PLACES = 8
TILE = 32
FOLD = 96
OWN = 64
EXT = 192
MIRROR = 104
PAD = 8


def chebyshev_in_powers():
    rows = [[1], [0, 1]]
    for _ in range(2, TERMS):
        up = [0] + [2 * v for v in rows[-1]]
        old = rows[-2] + [0] * (len(up) - len(rows[-2]))
        rows.append([a - b for a, b in zip(up, old)])
    return rows


def spans(low, high):
    marks = [low] + [m for m in (16, 32, 56, 64, 80) if m > low] + [high]
    return [(start, stop - start) for start, stop in zip(marks[:-1], marks[1:])]


def kernel(
    surface, speeds, table, out,
    field, stage, planes, raw, speed, rim, table_row, tab, indices,
    partial, beside, joined, landed, halo,
    local_sem, field_send, field_recv, speed_send, speed_recv, relay_send, rim_send, rim_recv,
    halo_send, halo_recv, beside_send, beside_recv, image_send, image_recv,
):
    s = lax.axis_index("depth")
    t = lax.axis_index("tile")
    columns = lax.axis_size("tile") // 2
    col, zl = t // 2, t % 2
    zh, core = s // 2, s % 2
    z = zh * 2 + zl
    freq = s * 2 + zl
    sibling = zh * 2 + (1 - core)
    has_left = col > 0
    has_right = col < columns - 1
    sides = ((0, has_left), (1, has_right))

    def chip(step):
        other = (z + step) % 8
        return other // 2, other % 2

    def rows(first, size):
        return pl.ds(pl.multiple_of(first, 8), size)

    lane = lax.broadcasted_iota(jnp.int32, (8, 128), 1)
    sub = lax.broadcasted_iota(jnp.int32, (8, 128), 0)
    low_half = lane < 64
    bit0, bit1 = sub % 2 == 0, (sub // 2) % 2 == 0
    parity = jnp.where(low_half, 2 * lane, 2 * lane - 127)
    interleave = lane // 2 + 64 * (lane % 2)
    wall = (sub == 7) & (
        (low_half & jnp.logical_not(has_left))
        | (jnp.logical_not(low_half) & jnp.logical_not(has_right))
    )
    tall = lax.broadcasted_iota(jnp.int32, (24, 128), 1) % 64
    first_lane, last_lane = tall == 0, tall == 63

    def swap(v):
        return pltpu.roll(v, 64, 1)

    def reverse(v):
        v = pltpu.roll(v, 4, 0)
        v = jnp.where(bit1, pltpu.roll(v, 6, 0), pltpu.roll(v, 2, 0))
        return jnp.where(bit0, pltpu.roll(v, 7, 0), pltpu.roll(v, 1, 0))

    def split(v):
        return jnp.take_along_axis(v, parity, axis=1, mode="promise_in_bounds")

    def join(top, low):
        return jnp.where(low_half, top, swap(low)), jnp.where(low_half, swap(top), low)

    def mirror(p, eo, v):
        planes[0, p, eo, PAD + FOLD : PAD + MIRROR, :] = reverse(swap(v))

    other_freq = s * 2 + 1 - zl
    local = (
        pltpu.make_async_copy(speeds, raw, local_sem.at[0]),
        pltpu.make_async_copy(
            surface.at[freq // 4, :, freq % 4],
            field.at[:, rows(OWN + TILE * zl, TILE), :],
            local_sem.at[1],
        ),
        pltpu.make_async_copy(
            surface.at[other_freq // 4, :, other_freq % 4], stage, local_sem.at[2]
        ),
        pltpu.make_async_copy(table.at[freq], table_row, local_sem.at[3]),
    )
    for copy in local:
        copy.start()

    for side, there in sides:

        @pl.when(jnp.logical_not(there))
        def _():
            base = 2 * OWN * side
            field[:, base : base + OWN, :] = jnp.zeros((4, OWN, 128), jnp.float32)
            rim[:, side] = jnp.zeros((LEVELS, 2, TILE, 128), jnp.int32)
            halo[side] = jnp.zeros((4, 2, TILE, 128), jnp.float32)

    barrier = pltpu.get_barrier_semaphore()

    def greet(depth, tile):
        pl.semaphore_signal(barrier, inc=1, device_id=(depth, tile), device_id_type=MESH)

    for step in range(4, 12):
        ozh, ozl = chip(step)
        if step != 8:
            greet(ozh * 2, 2 * col + ozl)
            greet(ozh * 2 + 1, 2 * col + ozl)

    for side, there in sides:

        @pl.when(there)
        def _():
            greet(s, 2 * (col - 1 + 2 * side))
            greet(s, 2 * (col - 1 + 2 * side) + 1)

    greet(sibling, t)

    for copy in local:
        copy.wait()

    coef = chebyshev_in_powers()
    for part in range(2):
        for power in range(TERMS):
            row = None
            for n in range(power, TERMS):
                c = coef[n][power]
                if c:
                    term = table_row[part, n : n + 1, :] * (c / 8.0**power)
                    row = term if row is None else row + term
            tab[part * TERMS + power] = jnp.broadcast_to(row, (8, 128))

    for lev in range(2):
        for r in range(0, TILE, 8):
            straight = split(raw[lev, r : r + 8, :])
            turned = reverse(split(raw[lev, 24 - r : TILE - r, :]))
            speed[2 * s + lev, zl, r : r + 8, :] = jnp.where(zl == 0, straight, turned)

    pl.semaphore_wait(
        barrier, 15 + 2 * has_left.astype(jnp.int32) + 2 * has_right.astype(jnp.int32)
    )

    def speed_copy(owner, owner_zl, target, sem):
        part = speed.at[pl.ds(2 * owner, 2), owner_zl]
        return pltpu.make_async_remote_copy(
            src_ref=part,
            dst_ref=part,
            send_sem=sem,
            recv_sem=speed_recv.at[owner, owner_zl],
            device_id=target,
            device_id_type=MESH,
        )

    def each_speed(action):
        for step in (4, 3, 5, 2, 6, 1, 7):
            ozh, ozl = chip(step)
            action(
                speed_copy(s, zl, (ozh * 2 + core, 2 * col + ozl), speed_send.at[step])
            )
        action(speed_copy(s, zl, (sibling, t), speed_send.at[0]))

    def relay(owner, owner_zl):
        return speed_copy(owner, owner_zl, (sibling, t), relay_send.at[owner // 2, owner_zl])

    def foreign(owner, owner_zl):
        return jnp.logical_not((owner == s) & (owner_zl == zl))

    def passes(owner, owner_zl):
        return foreign(owner, owner_zl) & (owner % 2 == core)

    def take_speeds(first, last):
        for owner in range(first, last):
            for owner_zl in range(2):

                @pl.when(passes(owner, owner_zl))
                def _():
                    relay(owner, owner_zl).wait_recv()
                    relay(owner, owner_zl).start()

        for owner in range(first, last):
            for owner_zl in range(2):

                @pl.when(owner % 2 != core)
                def _():
                    relay(owner, owner_zl).wait_recv()

    def start(copy):
        copy.start()

    def wait_send(copy):
        copy.wait_send()

    @pl.when(s == 0)
    def _():
        each_speed(start)

    def field_copy(source, target, row, sem):
        return pltpu.make_async_remote_copy(
            src_ref=source,
            dst_ref=field.at[:, rows(row, TILE), :],
            send_sem=field_send.at[sem],
            recv_sem=field_recv.at[row // TILE],
            device_id=(s, target),
            device_id_type=MESH,
        )

    own_field = field.at[:, rows(OWN + TILE * zl, TILE), :]
    inner = field_copy(stage, 2 * col + 1 - zl, OWN + TILE * zl, 0)

    def outer(side):
        target = 2 * (col - 1 + 2 * side)
        row = 2 * OWN * (1 - side) + TILE * zl
        return (
            field_copy(stage, target + 1 - zl, row, 1 + 2 * side),
            field_copy(own_field, target + zl, row, 2 + 2 * side),
        )

    inner.start()
    for side, there in sides:

        @pl.when(there)
        def _():
            for copy in outer(side):
                copy.start()

    field_copy(stage, t, OWN + TILE * (1 - zl), 0).wait_recv()
    for side, there in sides:

        @pl.when(there)
        def _():
            for part in range(2):
                field_copy(stage, t, 2 * OWN * side + TILE * part, 0).wait_recv()

    inner.wait_send()
    for side, there in sides:

        @pl.when(there)
        def _():
            for copy in outer(side):
                copy.wait_send()

    @pl.when(s > 0)
    def _():
        each_speed(start)

    def fold_plane(p, c):
        sign = jnp.where(p == 3, -1.0, 1.0)
        tops = [split(field[p, r : r + 8, :] * sign) for r in range(0, FOLD, 8)]
        lows = [split(reverse(field[p, EXT - 8 - r : EXT - r, :] * sign)) for r in range(0, FOLD, 8)]
        for j in range(FOLD // 8):
            for eo, v in enumerate(join(tops[j], lows[j])):
                planes[0, p, eo, PAD + 8 * j : PAD + 8 * j + 8, :] = v
                if j == FOLD // 8 - 1:
                    mirror(p, eo, v)
        return c

    lax.fori_loop(0, 4, fold_plane, 0)

    def velocity(level, r):
        if r >= OWN:
            at = r - OWN
            return join(speed[level, 0, at : at + 8, :], speed[level, 1, at : at + 8, :])
        if r >= TILE:
            at = OWN - 8 - r
            return join(
                reverse(rim[level, 0, 1, at : at + 8, :]),
                reverse(rim[level, 1, 0, at : at + 8, :]),
            )
        return join(rim[level, 0, 0, r : r + 8, :], rim[level, 1, 1, r : r + 8, :])

    def rim_copy(turn, place, side):
        level = PLACES * turn + place
        size = 8 * (7 - place)
        if size > TILE:
            source, target = speed.at[level], rim.at[level, 1 - side]
        else:
            source = speed.at[level, side, pl.ds(0, size), :]
            target = rim.at[level, 1 - side, side, pl.ds(0, size), :]
        return pltpu.make_async_remote_copy(
            src_ref=source,
            dst_ref=target,
            send_sem=rim_send.at[turn, place, side],
            recv_sem=rim_recv.at[turn, place, 1 - side],
            device_id=(s, t - 2 + 4 * side),
            device_id_type=MESH,
        )

    def each_rim(turn, places, action):
        for place in places:
            for side, there in sides:

                @pl.when(there)
                def _():
                    action(rim_copy(turn, place, side))

    def halo_copy(side):
        return pltpu.make_async_remote_copy(
            src_ref=planes.at[0].at[:, :, pl.ds(PAD + OWN, TILE), :],
            dst_ref=halo.at[1 - side],
            send_sem=halo_send.at[side],
            recv_sem=halo_recv.at[1 - side],
            device_id=(s, t - 2 + 4 * side),
            device_id_type=MESH,
        )

    def send_halo():
        for side, there in sides:

            @pl.when(there)
            def _():
                halo_copy(side).start()

    def take_halo():
        for side, there in sides:

            @pl.when(there)
            def _():
                halo_copy(1 - side).wait_recv()
                halo_copy(side).wait_send()

        def place_plane(p, c):
            for eo in range(2):
                for r in range(0, TILE, 8):
                    left = halo[0, p, eo, r : r + 8, :]
                    right = halo[1, p, eo, r : r + 8, :]
                    planes[0, p, eo, PAD + r : PAD + r + 8, :] = jnp.where(low_half, left, right)
                    far = PAD + OWN - 8 - r
                    planes[0, p, eo, far : far + 8, :] = reverse(
                        swap(jnp.where(low_half, right, left))
                    )
            return c

        lax.fori_loop(0, 4, place_plane, 0)

    def stencil(n, low, high):
        for p in range(4):
            for r, size in spans(low, high):
                at = PAD + r
                near, far = [], []
                for eo in range(2):
                    w = planes[n, p, eo, at : at + size, :]
                    ring = planes[n, p, eo, at - 1 : at + size - 1, :] + (
                        planes[n, p, eo, at + 1 : at + size + 1, :]
                    )
                    near.append(ring + (w + w))
                    far.append(ring - (w + w))
                left = jnp.where(first_lane[:size], 0.0, pltpu.roll(near[1], 1, 1))
                right = jnp.where(last_lane[:size], 0.0, pltpu.roll(near[0], 127, 1))
                both = (
                    (far[0] + far[0]) + (near[1] + left),
                    (far[1] + far[1]) + (near[0] + right),
                )
                for eo, g in enumerate(both):
                    if r == 56:
                        g = jnp.where(wall, 0.0, g)
                    planes[n + 1, p, eo, at : at + size, :] = g

    def beside_copy(level):
        return pltpu.make_async_remote_copy(
            src_ref=partial.at[level, 1 - core],
            dst_ref=beside.at[level],
            send_sem=beside_send.at[level],
            recv_sem=beside_recv.at[level],
            device_id=(sibling, t),
            device_id_type=MESH,
        )

    def image_copy(level):
        return pltpu.make_async_remote_copy(
            src_ref=joined.at[level],
            dst_ref=landed.at[level % 2, z],
            send_sem=image_send.at[level],
            recv_sem=image_recv.at[level % 2, z],
            device_id=(level // 2, 2 * col + core),
            device_id_type=MESH,
        )

    def mine(level):
        return (level // 2 == s) & (core == zl)

    def pass_on(level):
        beside_copy(level).wait_recv()
        total = partial[level, core] + beside[level]

        @pl.when(mine(level))
        def _():
            landed[level % 2, z] = total

        @pl.when(jnp.logical_not(mine(level)))
        def _():
            joined[level] = total
            image_copy(level).start()

    def advance(turn, place):
        low = 8 * (place + 1)
        level = PLACES * turn + place

        def find_indices():
            if place < PLACES - 1:
                for side, there in sides:

                    @pl.when(there)
                    def _():
                        rim_copy(turn, place, 1 - side).wait_recv()

            for r in range(low, FOLD, 8):
                for eo, index in enumerate(velocity(level, r)):
                    indices[eo, r : r + 8, :] = index

        if place:
            find_indices()
        for n in range(TERMS - 2):
            stencil(n, low - 8, MIRROR)
        stencil(TERMS - 2, low, FOLD)
        if not place:
            find_indices()
        for r in range(FOLD - 8, low - 8, -8):
            image = []
            for eo in range(2):
                index = indices[eo, r : r + 8, :]
                total = None
                for n in range(TERMS):
                    cos = jnp.take_along_axis(tab[n], index, axis=1, mode="promise_in_bounds")
                    sin = jnp.take_along_axis(
                        tab[TERMS + n], index, axis=1, mode="promise_in_bounds"
                    )
                    a, b, c, d = (planes[n, p, eo, PAD + r : PAD + r + 8, :] for p in range(4))
                    new = (
                        cos * a - sin * b,
                        cos * b + sin * a,
                        cos * c - sin * d,
                        cos * d + sin * c,
                    )
                    total = new if n == 0 else tuple(o + v for o, v in zip(total, new))
                for p in range(4):
                    planes[0, p, eo, PAD + r : PAD + r + 8, :] = total[p]
                    if r == FOLD - 8:
                        mirror(p, eo, total[p])
                image.append(total[0] * total[2] - total[1] * total[3])
            if r >= OWN:
                for half, v in enumerate(join(image[0], image[1])):
                    partial[level, half, r - OWN : r - OWN + 8, :] = v
        beside_copy(level).start()

        @pl.when(level > 0)
        def _():
            pass_on(level - 1)

    def run_turn(turn, carry):
        @pl.when(turn == 0)
        def _():
            take_speeds(0, 1)
            each_rim(0, (0, 1), start)
            for owner in range(1, 4):
                take_speeds(owner, owner + 1)
                each_rim(0, (2 * owner, 2 * owner + 1)[: 7 - 2 * owner], start)

        @pl.when(turn == 1)
        def _():
            send_halo()
            take_halo()

        for place in range(PLACES):
            advance(turn, place)
            if place == 3:

                @pl.when(turn == 0)
                def _():
                    take_speeds(4, 8)
                    each_rim(1, range(7), start)

        return carry

    lax.fori_loop(0, 2, run_turn, 0)
    pass_on(LEVELS - 1)

    for lev in range(2):
        for step in (0, 1, 7, 2, 6, 3, 5, 4):
            source = (z + step) % 8
            arrival = pltpu.make_async_remote_copy(
                src_ref=joined.at[0],
                dst_ref=landed.at[lev, source],
                send_sem=image_send.at[0],
                recv_sem=image_recv.at[lev, source],
                device_id=(s, t),
                device_id_type=MESH,
            )
            if step:
                arrival.wait_recv()
            else:

                @pl.when(core != zl)
                def _():
                    arrival.wait_recv()

        sums = []
        for r in range(0, TILE, 8):
            total = landed[lev, 0, r : r + 8, :]
            for source in range(1, 8):
                total = total + landed[lev, source, r : r + 8, :]
            sums.append(jnp.take_along_axis(total, interleave, axis=1, mode="promise_in_bounds"))
        for j in range(4):
            out[lev, 8 * j : 8 * j + 8, :] = jnp.where(zl == 0, sums[j], reverse(sums[3 - j]))

    each_speed(wait_send)
    for owner in range(8):
        for owner_zl in range(2):

            @pl.when(passes(owner, owner_zl))
            def _():
                relay(owner, owner_zl).wait_send()

    for turn in range(2):
        each_rim(turn, range(7), wait_send)

    def drain(level, carry):
        beside_copy(level).wait_send()

        @pl.when(jnp.logical_not(mine(level)))
        def _():
            image_copy(level).wait_send()

        return carry

    lax.fori_loop(0, LEVELS, drain, 0)


def body(surface, speeds, table):
    hbm = pl.BlockSpec(memory_space=pltpu.HBM)
    dma = pltpu.SemaphoreType.DMA

    def vmem(*shape, dtype=jnp.float32):
        return pltpu.VMEM(shape, dtype)

    return pl.pallas_call(
        kernel,
        out_shape=jax.ShapeDtypeStruct((2, TILE, 128), jnp.float32),
        in_specs=[hbm, hbm, hbm],
        out_specs=pl.BlockSpec(memory_space=pltpu.VMEM),
        scratch_shapes=[
            vmem(4, EXT, 128),
            vmem(4, TILE, 128),
            vmem(TERMS, 4, 2, MIRROR + 2 * PAD, 128),
            vmem(2, TILE, 128, dtype=jnp.int32),
            vmem(LEVELS, 2, TILE, 128, dtype=jnp.int32),
            vmem(LEVELS, 2, 2, TILE, 128, dtype=jnp.int32),
            vmem(2, TERMS, 128),
            vmem(2 * TERMS, 8, 128),
            vmem(2, FOLD, 128, dtype=jnp.int32),
            vmem(LEVELS, 2, TILE, 128),
            vmem(LEVELS, TILE, 128),
            vmem(LEVELS, TILE, 128),
            vmem(2, 8, TILE, 128),
            vmem(2, 4, 2, TILE, 128),
            dma((4,)),
            dma((5,)),
            dma((6,)),
            dma((8,)),
            dma((8, 2)),
            dma((4, 2)),
            dma((2, 7, 2)),
            dma((2, 7, 2)),
            dma((2,)),
            dma((2,)),
            dma((LEVELS,)),
            dma((LEVELS,)),
            dma((LEVELS,)),
            dma((2, 8)),
        ],
        compiler_params=pltpu.CompilerParams(
            collective_id=0, has_side_effects=True, vmem_limit_bytes=60 << 20
        ),
    )(surface, speeds, table)


def solution(mesh):
    def flat(surface, speeds, table):
        return body(surface.reshape(4, 4, 4, TILE, 128), speeds, table)

    return jax.shard_map(
        flat,
        mesh=mesh,
        in_specs=(P(None, None, None, None, "tile", None), P("depth", "tile", None), P()),
        out_specs=P("depth", "tile", None),
        check_vma=False,
    )
```

```python
import jax
import jax.numpy as jnp
from jax import lax
from jax.experimental import pallas as pl
from jax.experimental.pallas import tpu as pltpu
from jax.sharding import PartitionSpec as P

MESH = pl.DeviceIdType.MESH
TERMS = 8
LEVELS = 16
PLACES = 8
TILE = 32
FOLD = 96
OWN = 64
EXT = 192
MIRROR = 104
PAD = 8


def chebyshev_in_powers():
    rows = [[1], [0, 1]]
    for _ in range(2, TERMS):
        up = [0] + [2 * v for v in rows[-1]]
        old = rows[-2] + [0] * (len(up) - len(rows[-2]))
        rows.append([a - b for a, b in zip(up, old)])
    return rows


def spans(low, high):
    marks = [low] + [m for m in (16, 32, 56, 64, 80) if low < m < high] + [high]
    return [(start, stop - start) for start, stop in zip(marks[:-1], marks[1:])]


def kernel(
    surface, speeds, table, out,
    field, stage, planes, raw, speed, rim, table_row, tab, factors,
    partial, beside, joined, landed, halo,
    local_sem, field_send, field_recv, speed_send, speed_recv, relay_send, rim_send, rim_recv,
    halo_send, halo_recv, beside_send, beside_recv, image_send, image_recv,
):
    s = lax.axis_index("depth")
    t = lax.axis_index("tile")
    columns = lax.axis_size("tile") // 2
    col, zl = t // 2, t % 2
    zh, core = s // 2, s % 2
    z = zh * 2 + zl
    freq = s * 2 + zl
    sibling = zh * 2 + (1 - core)
    has_left = col > 0
    has_right = col < columns - 1
    sides = ((0, has_left), (1, has_right))

    def chip(step):
        other = (z + step) % 8
        return other // 2, other % 2

    def rows(first, size):
        return pl.ds(pl.multiple_of(first, 8), size)

    lane = lax.broadcasted_iota(jnp.int32, (8, 128), 1)
    sub = lax.broadcasted_iota(jnp.int32, (8, 128), 0)
    low_half = lane < 64
    bit0, bit1 = sub % 2 == 0, (sub // 2) % 2 == 0
    parity = jnp.where(low_half, 2 * lane, 2 * lane - 127)
    interleave = lane // 2 + 64 * (lane % 2)
    wall = (sub == 7) & (
        (low_half & jnp.logical_not(has_left))
        | (jnp.logical_not(low_half) & jnp.logical_not(has_right))
    )
    tall = lax.broadcasted_iota(jnp.int32, (24, 128), 1) % 64
    first_lane, last_lane = tall == 0, tall == 63

    def swap(v):
        return pltpu.roll(v, 64, 1)

    def reverse(v):
        v = pltpu.roll(v, 4, 0)
        v = jnp.where(bit1, pltpu.roll(v, 6, 0), pltpu.roll(v, 2, 0))
        return jnp.where(bit0, pltpu.roll(v, 7, 0), pltpu.roll(v, 1, 0))

    def split(v):
        return jnp.take_along_axis(v, parity, axis=1, mode="promise_in_bounds")

    def join(top, low):
        return jnp.where(low_half, top, swap(low)), jnp.where(low_half, swap(top), low)

    def mirror(p, eo, v):
        planes[0, p, eo, PAD + FOLD : PAD + MIRROR, :] = reverse(swap(v))

    other_freq = s * 2 + 1 - zl
    local = (
        pltpu.make_async_copy(speeds, raw, local_sem.at[0]),
        pltpu.make_async_copy(
            surface.at[freq // 4, :, freq % 4],
            field.at[:, rows(OWN + TILE * zl, TILE), :],
            local_sem.at[1],
        ),
        pltpu.make_async_copy(
            surface.at[other_freq // 4, :, other_freq % 4], stage, local_sem.at[2]
        ),
        pltpu.make_async_copy(table.at[freq], table_row, local_sem.at[3]),
    )
    for copy in local:
        copy.start()

    for side, there in sides:

        @pl.when(jnp.logical_not(there))
        def _():
            base = 2 * OWN * side
            field[:, base : base + OWN, :] = jnp.zeros((4, OWN, 128), jnp.float32)
            rim[:, side] = jnp.zeros((LEVELS, 2, TILE, 128), jnp.int32)
            halo[side] = jnp.zeros((4, 2, TILE, 128), jnp.float32)

    barrier = pltpu.get_barrier_semaphore()

    def greet(depth, tile):
        pl.semaphore_signal(barrier, inc=1, device_id=(depth, tile), device_id_type=MESH)

    for step in range(4, 12):
        ozh, ozl = chip(step)
        if step != 8:
            greet(ozh * 2, 2 * col + ozl)
            greet(ozh * 2 + 1, 2 * col + ozl)

    for side, there in sides:

        @pl.when(there)
        def _():
            greet(s, 2 * (col - 1 + 2 * side))
            greet(s, 2 * (col - 1 + 2 * side) + 1)

    greet(sibling, t)

    for copy in local:
        copy.wait()

    coef = chebyshev_in_powers()
    for part in range(2):
        for power in range(TERMS):
            row = None
            for n in range(power, TERMS):
                c = coef[n][power]
                if c:
                    term = table_row[part, n : n + 1, :] * (c / 8.0**power)
                    row = term if row is None else row + term
            tab[part * TERMS + power] = jnp.broadcast_to(row, (8, 128))

    for lev in range(2):
        for r in range(0, TILE, 8):
            straight = split(raw[lev, r : r + 8, :])
            turned = reverse(split(raw[lev, 24 - r : TILE - r, :]))
            speed[2 * s + lev, zl, r : r + 8, :] = jnp.where(zl == 0, straight, turned)

    pl.semaphore_wait(
        barrier, 15 + 2 * has_left.astype(jnp.int32) + 2 * has_right.astype(jnp.int32)
    )

    def speed_copy(owner, owner_zl, target, sem):
        part = speed.at[pl.ds(2 * owner, 2), owner_zl]
        return pltpu.make_async_remote_copy(
            src_ref=part,
            dst_ref=part,
            send_sem=sem,
            recv_sem=speed_recv.at[owner, owner_zl],
            device_id=target,
            device_id_type=MESH,
        )

    def each_speed(action):
        for step in (4, 3, 5, 2, 6, 1, 7):
            ozh, ozl = chip(step)
            action(
                speed_copy(s, zl, (ozh * 2 + core, 2 * col + ozl), speed_send.at[step])
            )
        action(speed_copy(s, zl, (sibling, t), speed_send.at[0]))

    def relay(owner, owner_zl):
        return speed_copy(owner, owner_zl, (sibling, t), relay_send.at[owner // 2, owner_zl])

    def foreign(owner, owner_zl):
        return jnp.logical_not((owner == s) & (owner_zl == zl))

    def passes(owner, owner_zl):
        return foreign(owner, owner_zl) & (owner % 2 == core)

    def take_speeds(first, last):
        for owner in range(first, last):
            for owner_zl in range(2):

                @pl.when(passes(owner, owner_zl))
                def _():
                    relay(owner, owner_zl).wait_recv()
                    relay(owner, owner_zl).start()

        for owner in range(first, last):
            for owner_zl in range(2):

                @pl.when(owner % 2 != core)
                def _():
                    relay(owner, owner_zl).wait_recv()

    def start(copy):
        copy.start()

    def wait_send(copy):
        copy.wait_send()

    @pl.when(s < 2)
    def _():
        each_speed(start)

    def field_copy(source, target, row, sem):
        return pltpu.make_async_remote_copy(
            src_ref=source,
            dst_ref=field.at[:, rows(row, TILE), :],
            send_sem=field_send.at[sem],
            recv_sem=field_recv.at[row // TILE],
            device_id=(s, target),
            device_id_type=MESH,
        )

    own_field = field.at[:, rows(OWN + TILE * zl, TILE), :]
    inner = field_copy(stage, 2 * col + 1 - zl, OWN + TILE * zl, 0)

    def outer(side):
        target = 2 * (col - 1 + 2 * side)
        row = 2 * OWN * (1 - side) + TILE * zl
        return (
            field_copy(stage, target + 1 - zl, row, 1 + 2 * side),
            field_copy(own_field, target + zl, row, 2 + 2 * side),
        )

    inner.start()
    for side, there in sides:

        @pl.when(there)
        def _():
            for copy in outer(side):
                copy.start()

    def rim_copy(turn, place, side):
        level = PLACES * turn + place
        size = 8 * (7 - place)
        if size > TILE:
            source, target = speed.at[level], rim.at[level, 1 - side]
        else:
            source = speed.at[level, side, pl.ds(0, size), :]
            target = rim.at[level, 1 - side, side, pl.ds(0, size), :]
        return pltpu.make_async_remote_copy(
            src_ref=source,
            dst_ref=target,
            send_sem=rim_send.at[turn, place, side],
            recv_sem=rim_recv.at[turn, place, 1 - side],
            device_id=(s, t - 2 + 4 * side),
            device_id_type=MESH,
        )

    def each_rim(turn, places, action):
        for place in places:
            for side, there in sides:

                @pl.when(there)
                def _():
                    action(rim_copy(turn, place, side))

    take_speeds(0, 1)
    each_rim(0, (0, 1), start)

    @pl.when((s > 1) & (s < 4))
    def _():
        each_speed(start)

    field_copy(stage, t, OWN + TILE * (1 - zl), 0).wait_recv()
    for side, there in sides:

        @pl.when(there)
        def _():
            for part in range(2):
                field_copy(stage, t, 2 * OWN * side + TILE * part, 0).wait_recv()

    inner.wait_send()
    for side, there in sides:

        @pl.when(there)
        def _():
            for copy in outer(side):
                copy.wait_send()

    for p in range(4):
        sign = -1.0 if p == 3 else 1.0
        tops = [split(field[p, r : r + 8, :] * sign) for r in range(0, FOLD, 8)]
        lows = [split(reverse(field[p, EXT - 8 - r : EXT - r, :] * sign)) for r in range(0, FOLD, 8)]
        for j in range(FOLD // 8):
            for eo, v in enumerate(join(tops[j], lows[j])):
                planes[0, p, eo, PAD + 8 * j : PAD + 8 * j + 8, :] = v
                if j == FOLD // 8 - 1:
                    mirror(p, eo, v)

    def velocity(level, r):
        if r >= OWN:
            at = r - OWN
            return join(speed[level, 0, at : at + 8, :], speed[level, 1, at : at + 8, :])
        if r >= TILE:
            at = OWN - 8 - r
            return join(
                reverse(rim[level, 0, 1, at : at + 8, :]),
                reverse(rim[level, 1, 0, at : at + 8, :]),
            )
        return join(rim[level, 0, 0, r : r + 8, :], rim[level, 1, 1, r : r + 8, :])

    def halo_copy(side):
        return pltpu.make_async_remote_copy(
            src_ref=planes.at[0].at[:, :, pl.ds(PAD + OWN, TILE), :],
            dst_ref=halo.at[1 - side],
            send_sem=halo_send.at[side],
            recv_sem=halo_recv.at[1 - side],
            device_id=(s, t - 2 + 4 * side),
            device_id_type=MESH,
        )

    def send_halo():
        for side, there in sides:

            @pl.when(there)
            def _():
                halo_copy(side).start()

    def take_halo():
        for side, there in sides:

            @pl.when(there)
            def _():
                halo_copy(1 - side).wait_recv()
                halo_copy(side).wait_send()

        for p in range(4):
            for eo in range(2):
                far = []
                for r in range(0, TILE, 8):
                    left = halo[0, p, eo, r : r + 8, :]
                    right = halo[1, p, eo, r : r + 8, :]
                    planes[0, p, eo, PAD + r : PAD + r + 8, :] = jnp.where(low_half, left, right)
                    far.append(swap(jnp.where(low_half, right, left)))
                for j, v in enumerate(far):
                    at = PAD + OWN - 8 - 8 * j
                    planes[0, p, eo, at : at + 8, :] = reverse(v)

    def stencil(n, low, high):
        for p in (slice(0, 2), slice(2, 4)):
            for r, size in spans(low, high):
                at = PAD + r
                near, far = [], []
                for eo in range(2):
                    w = planes[n, p, eo, at : at + size, :]
                    ring = planes[n, p, eo, at - 1 : at + size - 1, :] + (
                        planes[n, p, eo, at + 1 : at + size + 1, :]
                    )
                    near.append(ring + (w + w))
                    far.append(ring - (w + w))
                left = jnp.where(first_lane[:size], 0.0, pltpu.roll(near[1], 1, 2))
                right = jnp.where(last_lane[:size], 0.0, pltpu.roll(near[0], 127, 2))
                both = (
                    (far[0] + far[0]) + (near[1] + left),
                    (far[1] + far[1]) + (near[0] + right),
                )
                for eo, g in enumerate(both):
                    if r == 56:
                        g = jnp.where(wall, 0.0, g)
                    planes[n + 1, p, eo, at : at + size, :] = g

    def beside_copy(level):
        return pltpu.make_async_remote_copy(
            src_ref=partial.at[level, 1 - core],
            dst_ref=beside.at[level],
            send_sem=beside_send.at[level],
            recv_sem=beside_recv.at[level],
            device_id=(sibling, t),
            device_id_type=MESH,
        )

    def image_copy(level):
        return pltpu.make_async_remote_copy(
            src_ref=joined.at[level],
            dst_ref=landed.at[level % 2, z],
            send_sem=image_send.at[level],
            recv_sem=image_recv.at[level % 2, z],
            device_id=(level // 2, 2 * col + core),
            device_id_type=MESH,
        )

    def mine(level):
        return (level // 2 == s) & (core == zl)

    def pass_on(level):
        beside_copy(level).wait_recv()
        total = partial[level, core] + beside[level]

        @pl.when(mine(level))
        def _():
            landed[level % 2, z] = total

        @pl.when(jnp.logical_not(mine(level)))
        def _():
            joined[level] = total
            image_copy(level).start()

    def find_factors(turn, place):
        if place < PLACES - 1:
            for side, there in sides:

                @pl.when(there)
                def _():
                    rim_copy(turn, place, 1 - side).wait_recv()

        span = range(8 * (place + 1), FOLD, 8)
        pairs = [velocity(PLACES * turn + place, r) for r in span]
        for r, pair in zip(span, pairs):
            for eo in range(2):
                at = 2 * r + 8 * eo
                for n in range(2 * TERMS):
                    factors[place, n, at : at + 8, :] = jnp.take_along_axis(
                        tab[n], pair[eo], axis=1, mode="promise_in_bounds"
                    )

    def advance(turn, place):
        low = 8 * (place + 1)
        level = PLACES * turn + place

        for n in range(TERMS - 2):
            stencil(n, low - 8, MIRROR)
        stencil(TERMS - 2, low, FOLD)

        @pl.when(turn == 0)
        def _():
            if not place:
                take_speeds(1, 2)
                each_rim(0, (2, 3), start)

                @pl.when(s >= 4)
                def _():
                    each_speed(start)

            find_factors(turn, place)

        for r in range(FOLD - 8, low - 8, -8):
            image = []
            for eo in range(2):
                by_cos = by_sin = None
                at = 2 * r + 8 * eo
                for n in range(TERMS):
                    term = planes[n, :, eo, PAD + r : PAD + r + 8, :]
                    cos = factors[place, n, at : at + 8, :] * term
                    sin = factors[place, TERMS + n, at : at + 8, :] * term
                    by_cos = cos if n == 0 else by_cos + cos
                    by_sin = sin if n == 0 else by_sin + sin
                total = (
                    by_cos[0] - by_sin[1],
                    by_cos[1] + by_sin[0],
                    by_cos[2] - by_sin[3],
                    by_cos[3] + by_sin[2],
                )
                for p in range(4):
                    planes[0, p, eo, PAD + r : PAD + r + 8, :] = total[p]
                    if r == FOLD - 8:
                        mirror(p, eo, total[p])
                image.append(total[0] * total[2] - total[1] * total[3])
            if r >= OWN:
                for half, v in enumerate(join(image[0], image[1])):
                    partial[level, half, r - OWN : r - OWN + 8, :] = v
        if place == PLACES - 1:

            @pl.when(turn == 0)
            def _():
                send_halo()

        beside_copy(level).start()

        @pl.when(level > 0)
        def _():
            pass_on(level - 1)

    def run_turn(turn, carry):
        @pl.when(turn == 1)
        def _():
            for place in range(PLACES):
                find_factors(turn, place)
            take_halo()

        for place in range(PLACES):
            advance(turn, place)
            for after, first, last, round, places in (
                (0, 2, 3, 0, (4, 5)),
                (1, 3, 4, 0, (6,)),
                (3, 4, 8, 1, range(7)),
            ):
                if place == after:

                    @pl.when(turn == 0)
                    def _():
                        take_speeds(first, last)
                        each_rim(round, places, start)

        return carry

    lax.fori_loop(0, 2, run_turn, 0)
    pass_on(LEVELS - 1)

    for lev in range(2):
        for step in (0, 1, 7, 2, 6, 3, 5, 4):
            source = (z + step) % 8
            arrival = pltpu.make_async_remote_copy(
                src_ref=joined.at[0],
                dst_ref=landed.at[lev, source],
                send_sem=image_send.at[0],
                recv_sem=image_recv.at[lev, source],
                device_id=(s, t),
                device_id_type=MESH,
            )
            if step:
                arrival.wait_recv()
            else:

                @pl.when(core != zl)
                def _():
                    arrival.wait_recv()

        sums = []
        for r in range(0, TILE, 8):
            total = landed[lev, 0, r : r + 8, :]
            for source in range(1, 8):
                total = total + landed[lev, source, r : r + 8, :]
            sums.append(jnp.take_along_axis(total, interleave, axis=1, mode="promise_in_bounds"))
        for j in range(4):
            out[lev, 8 * j : 8 * j + 8, :] = jnp.where(zl == 0, sums[j], reverse(sums[3 - j]))

    each_speed(wait_send)
    for owner in range(8):
        for owner_zl in range(2):

            @pl.when(passes(owner, owner_zl))
            def _():
                relay(owner, owner_zl).wait_send()

    for turn in range(2):
        each_rim(turn, range(7), wait_send)

    def drain(level, carry):
        beside_copy(level).wait_send()

        @pl.when(jnp.logical_not(mine(level)))
        def _():
            image_copy(level).wait_send()

        return carry

    lax.fori_loop(0, LEVELS, drain, 0)


def body(surface, speeds, table):
    hbm = pl.BlockSpec(memory_space=pltpu.HBM)
    dma = pltpu.SemaphoreType.DMA

    def vmem(*shape, dtype=jnp.float32):
        return pltpu.VMEM(shape, dtype)

    return pl.pallas_call(
        kernel,
        out_shape=jax.ShapeDtypeStruct((2, TILE, 128), jnp.float32),
        in_specs=[hbm, hbm, hbm],
        out_specs=pl.BlockSpec(memory_space=pltpu.VMEM),
        scratch_shapes=[
            vmem(4, EXT, 128),
            vmem(4, TILE, 128),
            vmem(TERMS, 4, 2, MIRROR + 2 * PAD, 128),
            vmem(2, TILE, 128, dtype=jnp.int32),
            vmem(LEVELS, 2, TILE, 128, dtype=jnp.int32),
            vmem(LEVELS, 2, 2, TILE, 128, dtype=jnp.int32),
            vmem(2, TERMS, 128),
            vmem(2 * TERMS, 8, 128),
            vmem(PLACES, 2 * TERMS, 2 * FOLD, 128),
            vmem(LEVELS, 2, TILE, 128),
            vmem(LEVELS, TILE, 128),
            vmem(LEVELS, TILE, 128),
            vmem(2, 8, TILE, 128),
            vmem(2, 4, 2, TILE, 128),
            dma((4,)),
            dma((5,)),
            dma((6,)),
            dma((8,)),
            dma((8, 2)),
            dma((4, 2)),
            dma((2, 7, 2)),
            dma((2, 7, 2)),
            dma((2,)),
            dma((2,)),
            dma((LEVELS,)),
            dma((LEVELS,)),
            dma((LEVELS,)),
            dma((2, 8)),
        ],
        compiler_params=pltpu.CompilerParams(
            collective_id=0, has_side_effects=True, vmem_limit_bytes=60 << 20
        ),
    )(surface, speeds, table)


def solution(mesh):
    def flat(surface, speeds, table):
        return body(surface.reshape(4, 4, 4, TILE, 128), speeds, table)

    return jax.shard_map(
        flat,
        mesh=mesh,
        in_specs=(P(None, None, None, None, "tile", None), P("depth", "tile", None), P()),
        out_specs=P("depth", "tile", None),
        check_vma=False,
    )
```
